1024 devices in a mesh: section: 8 (over z_lo), ctx: 32 (over z_hi, x, core), tp: 4 (over y).
Axes of the slice: x: 4, y: 4, z: 32 (z_hi: 4, z_lo: 8; z = z_hi * 8 + z_lo), core: 2. Of those that a mesh axis runs over, the one named last changes fastest.
Arguments:
- queries: bfloat16 [8, 4096, 8192], P('section', 'ctx', 'tp'), may hold values from -80 to 80
- keys: bfloat16 [8, 4096, 1024], P('section', 'ctx', 'tp'), may hold values from -4 to 4
- values: bfloat16 [8, 4096, 1024], P('section', 'ctx', 'tp'), may hold values from -6 to 6
- span_order: int32 [64], replicated, may hold values from 0 to 63, as said below
Outputs:
- attended: bfloat16 [8, 4096, 8192], P('section', ('ctx', 'tp'))
The draws below stay inside these ranges and needn't reach their ends.
Inputs may be any that keep to these rules, and one draw needn't show every extreme that they name: `span_order`: a permutation of 0 to 63 in which entries 2 c and 2 c + 1 sum to 63 for every c.
All inputs are finite; a program needn't handle non-finite values.
Results may differ from the reference program's by a relative error of at most 0.0055.
Values may be sent and summed in bfloat16 or wider, within the bound.
No kernel may reach another device: no remote copies, remote signals or barrier semaphores. Data moves between devices by JAX's collectives and lax.ppermute only.
A program may use at most 32 MiB of HBM per device.

```python
import jax
import jax.numpy as jnp
from jax import lax

QUERY_HEADS = 64
KEY_VALUE_HEADS = 8
HEAD_DIMENSION = 128
TOK_DEV = 128
SEQUENCE_TOKENS = 4096
N_SECTION = 8
N_CTX = 32


def paired_order(key):
    folded = jax.random.fold_in(key, 11)
    shuffled = jax.random.permutation(folded, N_CTX).astype(jnp.int32)
    flipped = jax.random.randint(jax.random.fold_in(folded, 1), (N_CTX,), 0, 2).astype(jnp.int32)
    lower_half = shuffled
    upper_half = 2 * N_CTX - 1 - shuffled
    first_entry = jnp.where(flipped == 1, upper_half, lower_half)
    second_entry = jnp.where(flipped == 1, lower_half, upper_half)
    return jnp.stack([first_entry, second_entry], axis=1).reshape(2 * N_CTX).astype(jnp.int32)


def key_rows(key):
    unpermuted = jax.random.truncated_normal(jax.random.fold_in(key, 21), -4.0, 4.0, (N_SECTION, SEQUENCE_TOKENS, KEY_VALUE_HEADS * HEAD_DIMENSION), jnp.float32)
    return unpermuted


def draw_span_order(key, part):
    return paired_order(key)


def draw_keys(key, part):
    unpermuted = key_rows(key)
    return unpermuted.astype(jnp.bfloat16)


def draw_queries(key, part):
    result = jax.random.truncated_normal(jax.random.fold_in(key, 31), -4.0, 4.0, (N_SECTION, SEQUENCE_TOKENS, QUERY_HEADS * HEAD_DIMENSION), jnp.float32)
    return result.astype(jnp.bfloat16)


def level_of(rng, shape, cuts, low, largest):
    loudness, own = 1.0, jax.random.fold_in(rng, 6)
    for dim, shards_of in cuts:
        steps = jnp.exp(jax.random.uniform(jax.random.fold_in(own, dim), (shards_of,), jnp.float32, low / len(cuts), largest / len(cuts)))
        loudness = loudness * jnp.repeat(steps, shape[dim] // shards_of).reshape([-1 if axis == dim else 1 for axis in range(len(shape))])
    return loudness


def scatter_about(rng, dims, scale, limit, pieces=(), held_as=jnp.bfloat16):
    drawn = jax.random.normal(rng, dims, jnp.float32) * scale
    if len(pieces) > 0:
        drawn = level_of(rng, dims, pieces, -0.22, 0.18) * drawn
    return jnp.clip(drawn, min=-limit, max=limit).astype(held_as)


def setup_inputs(seed: int = 0) -> dict:
    streams_of = jax.random.split(jax.random.key(seed), 5)
    queries = draw_queries(jax.random.fold_in(streams_of[4], 71), 0)
    keys = draw_keys(jax.random.fold_in(streams_of[4], 71), 0)
    values = scatter_about(streams_of[2], (N_SECTION, SEQUENCE_TOKENS, KEY_VALUE_HEADS * HEAD_DIMENSION), 1.0, 6.0, ((0, 8), (1, 32), (2, 4)))
    span_order = draw_span_order(jax.random.fold_in(streams_of[4], 71), 0)
    return {"queries": queries, "keys": keys, "values": values, "span_order": span_order}


def token_positions(order):
    row_index = jnp.arange(SEQUENCE_TOKENS, dtype=jnp.int32)
    span_rows = TOK_DEV // 2
    return (order[row_index // span_rows] * span_rows + row_index % span_rows).astype(jnp.int32)

def reference(queries, keys, values, span_order):
    group_size = QUERY_HEADS // KEY_VALUE_HEADS
    received_queries = jnp.roll(queries, 1, axis=0)
    received_keys = jnp.roll(keys, 1, axis=0)
    received_values = jnp.roll(values, 1, axis=0)
    where_pos = token_positions(span_order)
    query_head_rows = received_queries.astype(jnp.float32).reshape(N_SECTION, SEQUENCE_TOKENS, KEY_VALUE_HEADS, group_size, HEAD_DIMENSION)
    query_head_rows = query_head_rows.transpose(0, 2, 1, 3, 4).reshape(N_SECTION * KEY_VALUE_HEADS, SEQUENCE_TOKENS, group_size, HEAD_DIMENSION)
    key_head_rows = received_keys.astype(jnp.float32).reshape(N_SECTION, SEQUENCE_TOKENS, KEY_VALUE_HEADS, HEAD_DIMENSION)
    key_head_rows = key_head_rows.transpose(0, 2, 1, 3).reshape(N_SECTION * KEY_VALUE_HEADS, SEQUENCE_TOKENS, HEAD_DIMENSION)
    value_head_rows = received_values.astype(jnp.float32).reshape(N_SECTION, SEQUENCE_TOKENS, KEY_VALUE_HEADS, HEAD_DIMENSION)
    value_head_rows = value_head_rows.transpose(0, 2, 1, 3).reshape(N_SECTION * KEY_VALUE_HEADS, SEQUENCE_TOKENS, HEAD_DIMENSION)
    score_scale = 1.0 / jnp.sqrt(jnp.float32(HEAD_DIMENSION))
    starts = jnp.arange(SEQUENCE_TOKENS // TOK_DEV, dtype=jnp.int32) * TOK_DEV

    def one_head(operands):
        head_q, head_k, head_v = operands

        def one_block(first_row):
            block_q = lax.dynamic_slice_in_dim(head_q, first_row, TOK_DEV, 0)
            block_pos = lax.dynamic_slice_in_dim(where_pos, first_row, TOK_DEV, 0)
            scores = jnp.einsum('qgd,sd->gqs', block_q, head_k, precision=lax.Precision.HIGHEST) * score_scale
            allowed = where_pos[None, :] <= block_pos[:, None]
            row_max = lax.optimization_barrier(jnp.max(jnp.where(allowed[None], scores, jnp.float32(-1e+30)), axis=-1))
            weights = jnp.where(allowed[None], jnp.exp(scores - row_max[..., None]), jnp.float32(0.0))
            denominator = lax.optimization_barrier(jnp.sum(weights, axis=-1))
            rounded = lax.optimization_barrier(weights.astype(jnp.bfloat16)).astype(jnp.float32)
            summed = jnp.einsum('gqs,sd->gqd', rounded, head_v, precision=lax.Precision.HIGHEST)
            result = summed / denominator[..., None]
            return result.transpose(1, 0, 2).astype(jnp.bfloat16)
        return lax.map(one_block, starts)
    block_list = lax.map(one_head, (query_head_rows, key_head_rows, value_head_rows))
    block_list = block_list.reshape(N_SECTION, KEY_VALUE_HEADS, SEQUENCE_TOKENS, group_size, HEAD_DIMENSION).transpose(0, 2, 1, 3, 4)
    return block_list.reshape(N_SECTION, SEQUENCE_TOKENS, QUERY_HEADS * HEAD_DIMENSION)
```

```python
import functools
import math

import jax
import jax.numpy as jnp
from jax import lax
from jax.experimental import pallas as pl
from jax.experimental.pallas import tpu as pltpu
from jax.sharding import PartitionSpec as P

HEAD = 128
SPAN = 64
GROUP = 8
SPANS = 64
BLOCK = 256
SCALE = math.log2(math.e) / math.sqrt(HEAD)
LOW = -1e30


def from_section_before(array, swap_cores):
    sections, ring = lax.axis_size("section"), lax.axis_size("ctx")
    pairs = [
        (s * ring + i, ((s + 1) % sections) * ring + (i ^ swap_cores))
        for s in range(sections)
        for i in range(ring)
    ]
    return lax.ppermute(array, ("section", "ctx"), pairs)


def along_x(array, by):
    pairs = [(i, (i // 8) * 8 + ((i % 8 // 2 + by) % 4) * 2 + i % 2) for i in range(32)]
    return lax.ppermute(array, "ctx", pairs)


def kernel(sources, first, last, order, own, other, *rest):
    rest = list(rest)
    chunks = [rest.pop(0) for _ in sources]
    if not first:
        acc_in, top_in, total_in = [rest.pop(0) for _ in range(3)]
    if last:
        out = rest.pop(0)
    acc, top, total = [rest.pop(0) for _ in range(3)]
    q_rows, k_sorted, v_sorted, held_by, row_of, place_of, counts = rest
    ctx = lax.axis_index("ctx")
    my_x, my_core = (ctx % 8) // 2, ctx % 2

    def place(i, carry):
        held_by[order[i]] = i
        return carry

    lax.fori_loop(0, SPANS, place, 0, unroll=8)

    def sort(p, filled):
        i = held_by[p]
        owner = i // 2
        source = (my_x - (owner % 8) // 2 + 4) % 4
        row = (owner // 8) * 256 + ((owner + my_core) % 2) * 128 + (i % 2) * SPAN
        updated = []
        for at, d in enumerate(sources):
            row_of[at, filled[at]] = row
            place_of[at, filled[at]] = p
            updated.append(filled[at] + (source == d).astype(jnp.int32))
            counts[at, p] = updated[at]
        return tuple(updated)

    lax.fori_loop(0, SPANS, sort, (jnp.int32(0),) * len(sources), unroll=4)

    places = []
    for j, ref in enumerate((own, other)):
        owner = ctx if j == 0 else ctx + 1 - 2 * my_core
        for e in range(2):
            places.append(order[2 * owner + e])
            for h in range(GROUP):
                q_rows[2 * j + e, h * SPAN : (h + 1) * SPAN, :] = ref[
                    e * SPAN : (e + 1) * SPAN, 2 * HEAD + h * HEAD : 2 * HEAD + (h + 1) * HEAD
                ]

    if first:
        acc[...] = jnp.zeros_like(acc)
        top[...] = jnp.full_like(top, LOW)
        total[...] = jnp.zeros_like(total)
    else:
        acc[...] = acc_in[...]
        top[...] = top_in[...]
        total[...] = total_in[...]

    width = GROUP * SPAN
    if 0 in sources:
        key_row = lax.broadcasted_iota(jnp.int32, (SPAN, width), 0)
        query_row = lax.broadcasted_iota(jnp.int32, (SPAN, width), 1) % SPAN
        later_by = key_row - query_row

    for at, (d, chunk) in enumerate(zip(sources, chunks)):
        for two in range(8):
            rows = [
                chunk[pl.ds(pl.multiple_of(row_of[at, 2 * two + u], SPAN), SPAN), :]
                for u in range(2)
            ]
            both = jnp.concatenate(rows, axis=0)
            k_sorted[at, two * 128 : (two + 1) * 128, :] = both[:, :HEAD]
            v_sorted[at, :, two * 128 : (two + 1) * 128] = both[:, HEAD:].T
        for j in range(2):
            low_spans = counts[at, places[2 * j]]
            high_spans = counts[at, places[2 * j + 1]]
            low_blocks = (low_spans + 3) // 4
            used, highs, valid, scores, starts = [], [], [], [], []
            for t in range(5):
                high = t >= low_blocks
                b = jnp.minimum(jnp.where(high, t - low_blocks, t), 3)
                spans = jnp.where(high, high_spans, low_spans)
                start = pl.multiple_of(b * BLOCK, BLOCK)
                s = 2 * j + high.astype(jnp.int32)
                block = lax.dot_general(
                    k_sorted[at, pl.ds(start, BLOCK), :],
                    q_rows[s],
                    (((1,), (1,)), ((), ())),
                    preferred_element_type=jnp.float32,
                )
                fresh = jnp.logical_or(jnp.logical_not(high), t - low_blocks < 4)
                for u in range(4):
                    part = block[u * SPAN : (u + 1) * SPAN]
                    if d == 0:
                        key_place = place_of[at, b * 4 + u]
                        slack = (jnp.where(high, places[2 * j + 1], places[2 * j]) - key_place) * SPAN
                        part = jnp.where(later_by <= slack, part, LOW)
                    scores.append(part.reshape(SPAN // 8, 8, width))
                    valid.append(jnp.logical_and(fresh, b * 4 + u < spans))
                    highs.append(high)
                used.append(s)
                starts.append(start)
            peaks = [jnp.max(part, axis=0) for part in scores]
            now, fade = [], []
            for e in range(2):
                peak = jnp.full((8, width), LOW, jnp.float32)
                for part, ok, high in zip(peaks, valid, highs):
                    ours = high if e else jnp.logical_not(high)
                    peak = jnp.maximum(peak, jnp.where(jnp.logical_and(ok, ours), part, LOW))
                peak = jnp.max(peak, axis=0, keepdims=True)
                before = top[2 * j + e]
                new = jnp.maximum(before, jnp.broadcast_to(peak, (8, width)))
                top[2 * j + e] = new
                now.append(new * SCALE)
                fade.append(jnp.exp2((before - new) * SCALE))
            for e in range(2):
                s = 2 * j + e
                acc[s] = (acc[s].reshape(HEAD // 8, 8, width) * fade[e][None]).reshape(HEAD, width)
                total[s] = total[s] * fade[e]
            for t in range(5):
                weights, added = [], jnp.zeros((8, width), jnp.float32)
                for u in range(4):
                    i = 4 * t + u
                    base = jnp.where(valid[i], jnp.where(highs[i], now[1], now[0]), -LOW)
                    w = jnp.exp2(scores[i] * SCALE - base[None])
                    added = added + jnp.sum(w, axis=0)
                    weights.append(w.reshape(SPAN, width).astype(jnp.bfloat16))
                total[used[t]] = total[used[t]] + added
                acc[used[t]] = acc[used[t]] + jnp.dot(
                    v_sorted[at, :, pl.ds(starts[t], BLOCK)],
                    jnp.concatenate(weights, axis=0),
                    preferred_element_type=jnp.float32,
                )

    if last:
        for j in range(2):
            core = my_core if j == 0 else 1 - my_core
            for e in range(2):
                s = 2 * j + e
                result = (acc[s] / jnp.sum(total[s], axis=0, keepdims=True)).T.astype(jnp.bfloat16)
                for f in range(2):
                    for h in range(GROUP):
                        at = h * SPAN + f * 32
                        out[core, 2 * e + f, :, h * HEAD : (h + 1) * HEAD] = result[at : at + 32]


def attend(order, own, other, chunks, sources, state=None, last=True):
    first = state is None
    state_shapes = (
        jax.ShapeDtypeStruct((4, HEAD, GROUP * SPAN), jnp.float32),
        jax.ShapeDtypeStruct((4, 8, GROUP * SPAN), jnp.float32),
        jax.ShapeDtypeStruct((4, 8, GROUP * SPAN), jnp.float32),
    )
    own_state = [pltpu.VMEM(s.shape, s.dtype) for s in state_shapes] if last else []
    n = len(chunks)
    scratch = own_state + [
        pltpu.VMEM((4, GROUP * SPAN, HEAD), jnp.bfloat16),
        pltpu.VMEM((n, 1024, HEAD), jnp.bfloat16),
        pltpu.VMEM((n, HEAD, 1024), jnp.bfloat16),
        pltpu.SMEM((SPANS,), jnp.int32),
        pltpu.SMEM((n, 17), jnp.int32),
        pltpu.SMEM((n, 17), jnp.int32),
        pltpu.SMEM((n, SPANS), jnp.int32),
    ]
    vmem = pl.BlockSpec(memory_space=pltpu.VMEM)
    inputs = [own, other, *chunks, *([] if first else state)]
    output = jax.ShapeDtypeStruct((2, 4, 32, GROUP * HEAD), jnp.bfloat16)
    pairs = n * 2 * 20 * SPAN * GROUP * SPAN
    return pl.pallas_call(
        functools.partial(kernel, tuple(sources), first, last),
        out_shape=output if last else state_shapes,
        in_specs=[pl.BlockSpec(memory_space=pltpu.SMEM)] + [vmem] * len(inputs),
        out_specs=vmem if last else (vmem,) * 3,
        scratch_shapes=scratch,
        compiler_params=pltpu.CompilerParams(vmem_limit_bytes=40 * 1024 * 1024),
        cost_estimate=pl.CostEstimate(
            flops=4 * pairs * HEAD, bytes_accessed=4 * 1024 * 1024, transcendentals=pairs
        ),
    )(order, *inputs)


def shards(queries, keys, values, span_order):
    core = lax.axis_index("ctx") % 2
    half = GROUP * HEAD
    heads = [
        jnp.concatenate(
            [a[0][:, h * HEAD : (h + 1) * HEAD] for a in (keys, values)]
            + [queries[0][:, h * half : (h + 1) * half]],
            axis=1,
        )
        for h in range(2)
    ]
    own, other = jnp.where(core == 0, heads[0], heads[1]), jnp.where(core == 0, heads[1], heads[0])
    own, other = from_section_before(own, 0), from_section_before(other, 1)
    chip_kv = jnp.concatenate([own[:, : 2 * HEAD], other[:, : 2 * HEAD]], axis=0)
    planes = [[z * 8 + r for z in range(4)] for r in range(8)]
    column = lax.all_gather(chip_kv, "ctx", axis=0, tiled=True, axis_index_groups=planes)
    chunks = {d: along_x(column, d) for d in (1, 3, 2)}
    state = attend(span_order, own, other, [column], (0,), last=False)
    state = attend(span_order, own, other, [chunks[1]], (1,), state, last=False)
    state = attend(span_order, own, other, [chunks[3]], (3,), state, last=False)
    out = attend(span_order, own, other, [chunks[2]], (2,), state)
    out = out.reshape(8, 32, half)
    peers = [[(chip * 2 + c) * 4 + y for c in range(2) for y in range(4)] for chip in range(16)]
    out = lax.all_to_all(
        out, ("ctx", "tp"), split_axis=0, concat_axis=0, tiled=True, axis_index_groups=peers
    )
    out = out.reshape(2, 4, 32, half).transpose(2, 1, 0, 3)
    return out.reshape(1, 32, 8 * half)


def solution(mesh):
    placed = (P("section", "ctx", "tp"), P("section", "ctx", "tp"), P("section", "ctx", "tp"), P())
    return jax.shard_map(
        shards,
        mesh=mesh,
        in_specs=placed,
        out_specs=P("section", ("ctx", "tp"), None),
        check_vma=False,
    )
```

```python
import functools
import math

import jax
import jax.numpy as jnp
from jax import lax
from jax.experimental import pallas as pl
from jax.experimental.pallas import tpu as pltpu
from jax.sharding import PartitionSpec as P

HEAD = 128
SPAN = 64
GROUP = 8
SPANS = 64
BLOCK = 256
SCALE = math.log2(math.e) / math.sqrt(HEAD)
LOW = -1e30
DIRECT = 384
PLACE, COUNT, MINE = 17, 34, 38


def between_cores(array):
    return lax.ppermute(array, "ctx", [(i, i ^ 1) for i in range(lax.axis_size("ctx"))])


def to_next_section(array, along_y):
    sections, peers = lax.axis_size("section"), lax.axis_size("tp")
    pairs = [
        (s * peers + y, ((s + 1) % sections) * peers + (y + along_y) % peers)
        for s in range(sections)
        for y in range(peers)
    ]
    return lax.ppermute(array, ("section", "tp"), pairs)


def along_x(array, by):
    pairs = [(i, (i // 8) * 8 + ((i % 8 // 2 + by) % 4) * 2 + i % 2) for i in range(32)]
    return lax.ppermute(array, "ctx", pairs)


def make_plan(order, plan, held_by, counts):
    ctx = lax.axis_index("ctx")
    my_x, my_core = (ctx >> 1) & 3, ctx & 1

    def place(i, carry):
        held_by[order[i]] = i
        return carry

    lax.fori_loop(0, SPANS, place, 0, unroll=8)

    def sort(p, filled):
        i = held_by[p]
        source = (my_x - (i >> 2)) & 3
        row = ((i >> 4) << 8) | ((((i >> 1) ^ my_core) & 1) << 7) | ((i & 1) << 6)
        updated = []
        for d in range(4):
            plan[d, filled[d]] = row
            plan[d, PLACE + filled[d]] = p
            updated.append(filled[d] + (source == d).astype(jnp.int32))
            counts[d, p] = updated[d]
        return tuple(updated)

    lax.fori_loop(0, SPANS, sort, (jnp.int32(0),) * 4, unroll=4)
    for j in range(2):
        owner = ctx if j == 0 else ctx + 1 - 2 * my_core
        for e in range(2):
            place = order[2 * owner + e]
            for d in range(4):
                plan[d, COUNT + 2 * j + e] = counts[d, place]
                plan[d, MINE + 2 * j + e] = place


def kernel(sources, groups, first, last, *refs):
    refs = list(refs)
    given, own, other = [refs.pop(0) for _ in range(3)]
    chunks = [[refs.pop(0) for _ in range(pieces)] for _, pieces in sources]
    if not first:
        acc_in, top_in, total_in = [refs.pop(0) for _ in range(3)]
    if last:
        out = refs.pop(0)
    acc, top, total = [refs.pop(0) for _ in range(3)]
    plan = refs.pop(0) if first else given
    q_rows, k_sorted, v_sorted = [refs.pop(0) for _ in range(3)]
    if first:
        make_plan(given, plan, *refs)
    places = [plan[0, MINE + s] for s in range(4)]
    for j in groups:
        ref = (own, other)[j]
        for e in range(2):
            for h in range(GROUP):
                q_rows[2 * j + e, h * SPAN : (h + 1) * SPAN, :] = ref[
                    e * SPAN : (e + 1) * SPAN, h * HEAD : (h + 1) * HEAD
                ]

    if first:
        acc[...] = jnp.zeros_like(acc)
        top[...] = jnp.full_like(top, LOW)
        total[...] = jnp.zeros_like(total)
    else:
        for j in groups:
            for ref, given in ((acc, acc_in), (top, top_in), (total, total_in)):
                ref[2 * j : 2 * j + 2] = given[2 * j : 2 * j + 2]

    width = GROUP * SPAN
    if first:
        key_row = lax.broadcasted_iota(jnp.int32, (SPAN, width), 0)
        query_row = lax.broadcasted_iota(jnp.int32, (SPAN, width), 1) % SPAN
        later_by = key_row - query_row

    for (source, pieces), chunk in zip(sources, chunks):
        if pieces == 1:
            chunk = chunk[0]
        else:
            whole, at = refs[0], 0
            for piece in chunk:
                whole[at : at + piece.shape[0], :] = piece[...]
                at += piece.shape[0]
            chunk = whole
        for two in range(8):
            rows = [
                chunk[pl.ds(pl.multiple_of(plan[source, 2 * two + u], SPAN), SPAN), :]
                for u in range(2)
            ]
            both = jnp.concatenate(rows, axis=0)
            k_sorted[two * 128 : (two + 1) * 128, :] = both[:, :HEAD]
            v_sorted[:, two * 128 : (two + 1) * 128] = both[:, HEAD:].T
        for j in groups:
            low_spans = plan[source, COUNT + 2 * j]
            high_spans = plan[source, COUNT + 2 * j + 1]
            low_blocks = (low_spans + 3) // 4
            used, highs, valid, scores, starts = [], [], [], [], []
            for t in range(5):
                high = t >= low_blocks
                b = jnp.minimum(jnp.where(high, t - low_blocks, t), 3)
                spans = jnp.where(high, high_spans, low_spans)
                start = pl.multiple_of(b * BLOCK, BLOCK)
                s = 2 * j + high.astype(jnp.int32)
                block = lax.dot_general(
                    k_sorted[pl.ds(start, BLOCK), :],
                    q_rows[s],
                    (((1,), (1,)), ((), ())),
                    preferred_element_type=jnp.float32,
                )
                fresh = jnp.logical_or(jnp.logical_not(high), t - low_blocks < 4)
                for u in range(4):
                    part = block[u * SPAN : (u + 1) * SPAN]
                    if first:
                        key_place = plan[source, PLACE + b * 4 + u]
                        mine = jnp.where(high, places[2 * j + 1], places[2 * j])
                        slack = (mine - key_place) * SPAN
                        part = jnp.where(later_by <= slack, part, LOW)
                    scores.append(part.reshape(SPAN // 8, 8, width))
                    valid.append(jnp.logical_and(fresh, b * 4 + u < spans))
                    highs.append(high)
                used.append(s)
                starts.append(start)
            peaks = [jnp.max(part, axis=0) for part in scores]
            now, fade = [], []
            for e in range(2):
                peak = jnp.full((8, width), LOW, jnp.float32)
                for part, ok, high in zip(peaks, valid, highs):
                    ours = high if e else jnp.logical_not(high)
                    peak = jnp.maximum(peak, jnp.where(jnp.logical_and(ok, ours), part, LOW))
                peak = jnp.max(peak, axis=0, keepdims=True)
                before = top[2 * j + e]
                new = jnp.maximum(before, jnp.broadcast_to(peak, (8, width)))
                top[2 * j + e] = new
                now.append(new * SCALE)
                fade.append(jnp.exp2((before - new) * SCALE))
            for e in range(2):
                s = 2 * j + e
                acc[s] = (acc[s].reshape(HEAD // 8, 8, width) * fade[e][None]).reshape(HEAD, width)
                total[s] = total[s] * fade[e]
            for t in range(5):
                weights, added = [], jnp.zeros((8, width), jnp.float32)
                for u in range(4):
                    i = 4 * t + u
                    base = jnp.where(valid[i], jnp.where(highs[i], now[1], now[0]), -LOW)
                    w = jnp.exp2(scores[i] * SCALE - base[None])
                    added = added + jnp.sum(w, axis=0)
                    weights.append(w.reshape(SPAN, width).astype(jnp.bfloat16))
                total[used[t]] = total[used[t]] + added
                acc[used[t]] = acc[used[t]] + jnp.dot(
                    v_sorted[:, pl.ds(starts[t], BLOCK)],
                    jnp.concatenate(weights, axis=0),
                    preferred_element_type=jnp.float32,
                )

    if last:
        my_y = lax.axis_index("tp")
        (j,) = groups
        for e in range(2):
            inverse = 1.0 / jnp.sum(total[2 * j + e], axis=0, keepdims=True)
            result = (acc[2 * j + e] * inverse).T.astype(jnp.bfloat16)
            for f in range(2):
                for h in range(GROUP):
                    at = h * SPAN + f * 32
                    out[(2 * e + f - my_y) & 3, :, h * HEAD : (h + 1) * HEAD] = result[at : at + 32]


def join(*refs):
    *pieces, out = refs
    for d, piece in enumerate(pieces):
        at = pl.multiple_of(((lax.axis_index("tp") - d) & 3) * piece.shape[1], HEAD)
        out[:, pl.ds(at, piece.shape[1])] = piece[...]


def attend(plan, own, other, chunks, state=None, groups=(0, 1), last=False):
    first = state is None
    state_shapes = (
        jax.ShapeDtypeStruct((4, HEAD, GROUP * SPAN), jnp.float32),
        jax.ShapeDtypeStruct((4, 8, GROUP * SPAN), jnp.float32),
        jax.ShapeDtypeStruct((4, 8, GROUP * SPAN), jnp.float32),
    )
    vmem, smem = pl.BlockSpec(memory_space=pltpu.VMEM), pl.BlockSpec(memory_space=pltpu.SMEM)
    scratch = [pltpu.VMEM(s.shape, s.dtype) for s in state_shapes] if last else []
    scratch += [
        pltpu.VMEM((4, GROUP * SPAN, HEAD), jnp.bfloat16),
        pltpu.VMEM((1024, HEAD), jnp.bfloat16),
        pltpu.VMEM((HEAD, 1024), jnp.bfloat16),
    ]
    if first:
        scratch += [pltpu.SMEM((SPANS,), jnp.int32), pltpu.SMEM((4, SPANS), jnp.int32)]
    sources = tuple((source, len(pieces)) for source, pieces in chunks)
    if any(pieces > 1 for _, pieces in sources):
        scratch += [pltpu.VMEM((1024, 2 * HEAD), jnp.bfloat16)]
    arrived = [piece for _, pieces in chunks for piece in pieces]
    inputs = [own, other, *arrived, *([] if first else state)]
    if last:
        shapes, specs = jax.ShapeDtypeStruct((4, 32, GROUP * HEAD), jnp.bfloat16), vmem
    else:
        shapes, specs = state_shapes, (vmem,) * 3
        if first:
            shapes, specs = (*shapes, jax.ShapeDtypeStruct((4, 64), jnp.int32)), (*specs, smem)
    pairs = len(sources) * len(groups) * 20 * SPAN * GROUP * SPAN
    return pl.pallas_call(
        functools.partial(kernel, sources, groups, first, last),
        out_shape=shapes,
        in_specs=[smem] + [vmem] * len(inputs),
        out_specs=specs,
        scratch_shapes=scratch,
        compiler_params=pltpu.CompilerParams(vmem_limit_bytes=24 * 1024 * 1024),
        cost_estimate=pl.CostEstimate(
            flops=4 * pairs * HEAD, bytes_accessed=4 * 1024 * 1024, transcendentals=pairs
        ),
    )(plan, *inputs)


def shards(queries, keys, values, span_order):
    core = lax.axis_index("ctx") % 2
    half = GROUP * HEAD
    kv = [
        jnp.concatenate([a[0][:, h * HEAD : (h + 1) * HEAD] for a in (keys, values)], axis=1)
        for h in range(2)
    ]
    q = (queries[0][:, :half], queries[0][:, half:])
    kv_own, kv_other = jnp.where(core == 0, kv[0], kv[1]), jnp.where(core == 0, kv[1], kv[0])
    own, other = jnp.where(core == 0, q[0], q[1]), jnp.where(core == 0, q[1], q[0])
    chip_kv = jnp.concatenate([kv_own, between_cores(kv_other)], axis=0)
    other = between_cores(other)
    planes = [[z * 8 + r for z in range(4)] for r in range(8)]
    column = lax.all_gather(chip_kv, "ctx", axis=0, tiled=True, axis_index_groups=planes)
    column, own, other = lax.optimization_barrier((column, own, other))
    back, ahead = along_x(column, 3), along_x(column, 1)
    straight = along_x(column[:DIRECT], 2)
    *state, plan = attend(span_order, own, other, [(0, [column])])
    back, *state = lax.optimization_barrier((back, *state))
    relayed = along_x(back[DIRECT:], 3)
    state = attend(plan, own, other, [(3, [back]), (1, [ahead])], state)
    last = ([(2, [straight, relayed])], state)
    out_other = between_cores(attend(plan, own, other, *last, groups=(1,), last=True))
    out_own = attend(plan, own, other, *last, groups=(0,), last=True)
    out = jnp.where(
        core == 0,
        jnp.concatenate([out_own, out_other], axis=2),
        jnp.concatenate([out_other, out_own], axis=2),
    )
    pieces = [to_next_section(out[d], d) for d in range(4)]
    vmem = pl.BlockSpec(memory_space=pltpu.VMEM)
    return pl.pallas_call(
        join,
        out_shape=jax.ShapeDtypeStruct((32, 4 * 2 * half), jnp.bfloat16),
        in_specs=[vmem] * 4,
        out_specs=vmem,
        compiler_params=pltpu.CompilerParams(vmem_limit_bytes=4 * 1024 * 1024),
    )(*pieces)[None]


def solution(mesh):
    placed = (P("section", "ctx", "tp"), P("section", "ctx", "tp"), P("section", "ctx", "tp"), P())
    return jax.shard_map(
        shards,
        mesh=mesh,
        in_specs=placed,
        out_specs=P("section", ("ctx", "tp"), None),
        check_vma=False,
    )
```

```python
import functools
import math

import jax
import jax.numpy as jnp
from jax import lax
from jax.experimental import pallas as pl
from jax.experimental.pallas import tpu as pltpu
from jax.sharding import PartitionSpec as P

HEAD = 128
SPAN = 64
GROUP = 8
SPANS = 64
BLOCK = 256
SCALE = math.log2(math.e) / math.sqrt(HEAD)
LOW = -1e30
DIRECT = 384
PLACE, COUNT, MINE = 17, 34, 38


def between_cores(array):
    return lax.ppermute(array, "ctx", [(i, i ^ 1) for i in range(lax.axis_size("ctx"))])


def to_next_section(array, along_y):
    sections, peers = lax.axis_size("section"), lax.axis_size("tp")
    pairs = [
        (s * peers + y, ((s + 1) % sections) * peers + (y + along_y) % peers)
        for s in range(sections)
        for y in range(peers)
    ]
    return lax.ppermute(array, ("section", "tp"), pairs)


def along_x(array, by):
    pairs = [(i, (i // 8) * 8 + ((i % 8 // 2 + by) % 4) * 2 + i % 2) for i in range(32)]
    return lax.ppermute(array, "ctx", pairs)


def make_plan(order, plan, held_by, counts):
    ctx = lax.axis_index("ctx")
    my_x, my_core = (ctx >> 1) & 3, ctx & 1

    def place(i, carry):
        held_by[order[i]] = i
        return carry

    lax.fori_loop(0, SPANS, place, 0, unroll=32)

    def sort(p, filled):
        i = held_by[p]
        source = (my_x - (i >> 2)) & 3
        row = ((i >> 4) << 8) | ((((i >> 1) ^ my_core) & 1) << 7) | ((i & 1) << 6)
        updated = []
        for d in range(4):
            plan[d, filled[d]] = row
            plan[d, PLACE + filled[d]] = p
            updated.append(filled[d] + (source == d).astype(jnp.int32))
            counts[d, p] = updated[d]
        return tuple(updated)

    lax.fori_loop(0, SPANS, sort, (jnp.int32(0),) * 4, unroll=16)
    for j in range(2):
        owner = ctx if j == 0 else ctx + 1 - 2 * my_core
        for e in range(2):
            place = order[2 * owner + e]
            for d in range(4):
                plan[d, COUNT + 2 * j + e] = counts[d, place]
                plan[d, MINE + 2 * j + e] = place


def kernel(sources, groups, first, last, *refs):
    refs = list(refs)
    given, own, other = [refs.pop(0) for _ in range(3)]
    chunks = [[refs.pop(0) for _ in range(pieces)] for _, pieces in sources]
    if not first:
        acc_in, top_in, total_in = [refs.pop(0) for _ in range(3)]
    if last:
        out = refs.pop(0)
    acc, top, total = [refs.pop(0) for _ in range(3)]
    plan = refs.pop(0) if first else given
    q_rows, k_sorted, v_sorted = [refs.pop(0) for _ in range(3)]
    if first:
        make_plan(given, plan, *refs)
    places = [plan[0, MINE + s] for s in range(4)]
    for j in groups:
        ref = (own, other)[j]
        for e in range(2):
            for h in range(GROUP):
                q_rows[2 * j + e, h * SPAN : (h + 1) * SPAN, :] = ref[
                    e * SPAN : (e + 1) * SPAN, h * HEAD : (h + 1) * HEAD
                ]

    if first:
        acc[...] = jnp.zeros_like(acc)
        top[...] = jnp.full_like(top, LOW)
        total[...] = jnp.zeros_like(total)
    else:
        for j in groups:
            for ref, given in ((top, top_in), (total, total_in)):
                ref[2 * j : 2 * j + 2] = given[2 * j : 2 * j + 2]

    width = GROUP * SPAN
    if first:
        key_row = lax.broadcasted_iota(jnp.int32, (SPAN, width), 0)
        query_row = lax.broadcasted_iota(jnp.int32, (SPAN, width), 1) % SPAN
        later_by = key_row - query_row

    for n, ((source, pieces), chunk) in enumerate(zip(sources, chunks)):
        held = acc if first or n > 0 else acc_in
        if pieces == 1:
            chunk = chunk[0]
        else:
            whole, at = refs[0], 0
            for piece in chunk:
                whole[at : at + piece.shape[0], :] = piece[...]
                at += piece.shape[0]
            chunk = whole
        for two in range(8):
            rows = [
                chunk[pl.ds(pl.multiple_of(plan[source, 2 * two + u], SPAN), SPAN), :]
                for u in range(2)
            ]
            both = jnp.concatenate(rows, axis=0)
            k_sorted[two * 128 : (two + 1) * 128, :] = both[:, :HEAD]
            v_sorted[:, two * 128 : (two + 1) * 128] = both[:, HEAD:].T
        for j in groups:
            low_spans = plan[source, COUNT + 2 * j]
            high_spans = plan[source, COUNT + 2 * j + 1]
            low_blocks = (low_spans + 3) // 4
            used, highs, valid, scores, starts = [], [], [], [], []
            for t in range(5):
                high = t >= low_blocks
                b = jnp.minimum(jnp.where(high, t - low_blocks, t), 3)
                spans = jnp.where(high, high_spans, low_spans)
                start = pl.multiple_of(b * BLOCK, BLOCK)
                s = 2 * j + high.astype(jnp.int32)
                block = lax.dot_general(
                    k_sorted[pl.ds(start, BLOCK), :],
                    q_rows[s],
                    (((1,), (1,)), ((), ())),
                    preferred_element_type=jnp.float32,
                )
                fresh = jnp.logical_or(jnp.logical_not(high), t - low_blocks < 4)
                for u in range(4):
                    part = block[u * SPAN : (u + 1) * SPAN]
                    if first:
                        key_place = plan[source, PLACE + b * 4 + u]
                        mine = jnp.where(high, places[2 * j + 1], places[2 * j])
                        slack = (mine - key_place) * SPAN
                        part = jnp.where(later_by <= slack, part, LOW)
                    scores.append(part.reshape(SPAN // 8, 8, width))
                    valid.append(jnp.logical_and(fresh, b * 4 + u < spans))
                    highs.append(high)
                used.append(s)
                starts.append(start)
            peaks = [jnp.max(part, axis=0) for part in scores]
            now, fade = [], []
            for e in range(2):
                peak = jnp.full((8, width), LOW, jnp.float32)
                for part, ok, high in zip(peaks, valid, highs):
                    ours = high if e else jnp.logical_not(high)
                    peak = jnp.maximum(peak, jnp.where(jnp.logical_and(ok, ours), part, LOW))
                peak = jnp.max(peak, axis=0, keepdims=True)
                before = top[2 * j + e]
                new = jnp.maximum(before, jnp.broadcast_to(peak, (8, width)))
                top[2 * j + e] = new
                now.append(new * SCALE)
                fade.append(jnp.exp2((before - new) * SCALE))
            for e in range(2):
                s = 2 * j + e
                faded = held[s].reshape(HEAD // 8, 8, width) * fade[e][None]
                acc[s] = faded.reshape(HEAD, width)
                total[s] = total[s] * fade[e]
            for t in range(5):
                weights, added = [], jnp.zeros((8, width), jnp.float32)
                for u in range(4):
                    i = 4 * t + u
                    base = jnp.where(valid[i], jnp.where(highs[i], now[1], now[0]), -LOW)
                    w = jnp.exp2(scores[i] * SCALE - base[None])
                    added = added + jnp.sum(w, axis=0)
                    weights.append(w.reshape(SPAN, width).astype(jnp.bfloat16))
                total[used[t]] = total[used[t]] + added
                acc[used[t]] = acc[used[t]] + jnp.dot(
                    v_sorted[:, pl.ds(starts[t], BLOCK)],
                    jnp.concatenate(weights, axis=0),
                    preferred_element_type=jnp.float32,
                )

    if last:
        my_y = lax.axis_index("tp")
        (j,) = groups
        for e in range(2):
            inverse = 1.0 / jnp.sum(total[2 * j + e], axis=0, keepdims=True)
            result = (acc[2 * j + e] * inverse).T.astype(jnp.bfloat16)
            for f in range(2):
                for h in range(GROUP):
                    at = h * SPAN + f * 32
                    out[(2 * e + f - my_y) & 3, :, h * HEAD : (h + 1) * HEAD] = result[at : at + 32]


def join(*refs):
    *pieces, out = refs
    for d, piece in enumerate(pieces):
        at = pl.multiple_of(((lax.axis_index("tp") - d) & 3) * piece.shape[1], HEAD)
        out[:, pl.ds(at, piece.shape[1])] = piece[...]


def attend(plan, own, other, chunks, state=None, groups=(0, 1), last=False):
    first = state is None
    state_shapes = (
        jax.ShapeDtypeStruct((4, HEAD, GROUP * SPAN), jnp.float32),
        jax.ShapeDtypeStruct((4, 8, GROUP * SPAN), jnp.float32),
        jax.ShapeDtypeStruct((4, 8, GROUP * SPAN), jnp.float32),
    )
    vmem, smem = pl.BlockSpec(memory_space=pltpu.VMEM), pl.BlockSpec(memory_space=pltpu.SMEM)
    scratch = [pltpu.VMEM(s.shape, s.dtype) for s in state_shapes] if last else []
    scratch += [
        pltpu.VMEM((4, GROUP * SPAN, HEAD), jnp.bfloat16),
        pltpu.VMEM((1024, HEAD), jnp.bfloat16),
        pltpu.VMEM((HEAD, 1024), jnp.bfloat16),
    ]
    if first:
        scratch += [pltpu.SMEM((SPANS,), jnp.int32), pltpu.SMEM((4, SPANS), jnp.int32)]
    sources = tuple((source, len(pieces)) for source, pieces in chunks)
    if any(pieces > 1 for _, pieces in sources):
        scratch += [pltpu.VMEM((1024, 2 * HEAD), jnp.bfloat16)]
    arrived = [piece for _, pieces in chunks for piece in pieces]
    inputs = [own, other, *arrived, *([] if first else state)]
    if last:
        shapes, specs = jax.ShapeDtypeStruct((4, 32, GROUP * HEAD), jnp.bfloat16), vmem
    else:
        shapes, specs = state_shapes, (vmem,) * 3
        if first:
            shapes, specs = (*shapes, jax.ShapeDtypeStruct((4, 64), jnp.int32)), (*specs, smem)
    pairs = len(sources) * len(groups) * 20 * SPAN * GROUP * SPAN
    return pl.pallas_call(
        functools.partial(kernel, sources, groups, first, last),
        out_shape=shapes,
        in_specs=[smem] + [vmem] * len(inputs),
        out_specs=specs,
        scratch_shapes=scratch,
        compiler_params=pltpu.CompilerParams(vmem_limit_bytes=24 * 1024 * 1024),
        cost_estimate=pl.CostEstimate(
            flops=4 * pairs * HEAD, bytes_accessed=4 * 1024 * 1024, transcendentals=pairs
        ),
    )(plan, *inputs)


def shards(queries, keys, values, span_order):
    core = lax.axis_index("ctx") % 2
    half = GROUP * HEAD
    kv = [
        jnp.concatenate([a[0][:, h * HEAD : (h + 1) * HEAD] for a in (keys, values)], axis=1)
        for h in range(2)
    ]
    q = (queries[0][:, :half], queries[0][:, half:])
    kv_own, kv_other = jnp.where(core == 0, kv[0], kv[1]), jnp.where(core == 0, kv[1], kv[0])
    own, other = jnp.where(core == 0, q[0], q[1]), jnp.where(core == 0, q[1], q[0])
    chip_kv = jnp.concatenate([kv_own, between_cores(kv_other)], axis=0)
    other = between_cores(other)
    planes = [[z * 8 + r for z in range(4)] for r in range(8)]
    column = lax.all_gather(chip_kv, "ctx", axis=0, tiled=True, axis_index_groups=planes)
    column, own, other = lax.optimization_barrier((column, own, other))
    back, ahead = along_x(column, 3), along_x(column, 1)
    straight = along_x(column[:DIRECT], 2)
    *state, plan = attend(span_order, own, other, [(0, [column])])
    back, *state = lax.optimization_barrier((back, *state))
    relayed = along_x(back[DIRECT:], 3)
    state = attend(plan, own, other, [(3, [back]), (1, [ahead])], state)
    last = ([(2, [straight, relayed])], state)
    out_other = between_cores(attend(plan, own, other, *last, groups=(1,), last=True))
    out_own = attend(plan, own, other, *last, groups=(0,), last=True)
    out = jnp.where(
        core == 0,
        jnp.concatenate([out_own, out_other], axis=2),
        jnp.concatenate([out_other, out_own], axis=2),
    )
    pieces = [to_next_section(out[d], d) for d in range(4)]
    vmem = pl.BlockSpec(memory_space=pltpu.VMEM)
    return pl.pallas_call(
        join,
        out_shape=jax.ShapeDtypeStruct((32, 4 * 2 * half), jnp.bfloat16),
        in_specs=[vmem] * 4,
        out_specs=vmem,
        compiler_params=pltpu.CompilerParams(vmem_limit_bytes=4 * 1024 * 1024),
    )(*pieces)[None]


def solution(mesh):
    placed = (P("section", "ctx", "tp"), P("section", "ctx", "tp"), P("section", "ctx", "tp"), P())
    return jax.shard_map(
        shards,
        mesh=mesh,
        in_specs=placed,
        out_specs=P("section", ("ctx", "tp"), None),
        check_vma=False,
    )
```
